32 devices in a mesh: groups: 2 (over x), team: 2 (over core), blk: 8 (over z, y).
Axes of the slice: x: 2, y: 2, z: 4, core: 2. Of those that a mesh axis runs over, the one named last changes fastest.
Arguments:
- probe: bfloat16 [192, 32, 128], P(('groups', 'blk')), parts along dimension 0, may hold values from -6 to 6
- positions: float32 [192, 3, 128], P(('groups', 'blk')), parts along dimension 0, as said below
- conductivity: float32 [192, 128], P(('groups', 'blk')), parts along dimension 0, may hold values from 0.5 to 2
- fluid_exchange: float32 [192, 128], P(('groups', 'blk')), parts along dimension 0, may hold values from 0.5 to 8
- row_blocks: int32 [192], P(('groups', 'blk')), parts along dimension 0, may hold values from 1 to 27, 864 in all
- column_blocks: int32 [192, 27], P(('groups', 'blk')), parts along dimension 0, may hold values from 0 to 95, as said below
Outputs:
- filtered: float32 [192, 32, 128], P(('groups', 'blk')), parts along dimension 0
The draws below stay inside these ranges and needn't reach their ends.
There are 2 independent parts, one for each index of `groups`. The reference program is written for one: setup_inputs(seed, part) draws one part's arguments, and reference() takes and returns one part's arrays. A program takes and returns all parts, laid end to end along the dimension named above; each array names one. Nothing has to cross between parts.
Inputs may be any that keep to these rules, and one draw needn't show every extreme that they name: `row_blocks`: every row lists at least one block; the counts of one bed sum to 864. `column_blocks`: ids in slots at or beyond a row's count are ignored; ids may repeat within a row. Every id differs from its row I by at most 24 around the closed order of the 96 clusters (J = (I + d) mod 96, |d| <= 24), and both ends of that reach occur. `positions`: clusters close in index lie close in space.
All inputs are finite; a program needn't handle non-finite values.
Results may differ from the reference program's by a relative error of at most 0.0029.
Values may be sent and summed in bfloat16 or wider, within the bound.
A program may use at most 64 MiB of HBM per device.

```python
import math
import jax
import jax.numpy as jnp
import numpy as np
from jax import lax

CL = 128
PROBE = 32
CT = 12
MAXB = 27
MEANB = 9
DEGREE = 8
NC = 96


def draw_column_blocks(key, part):
    reach = 2 * CT
    offsets = jax.random.randint(jax.random.fold_in(key, 11), (NC, MAXB), -reach, reach + 1)
    first_row = jax.random.randint(jax.random.fold_in(key, 12), (), 0, NC)
    second_row = (first_row + 1) % NC
    rows = jnp.arange(NC, dtype=jnp.int32)
    slot_zero = (jnp.arange(MAXB, dtype=jnp.int32) == 0)[None, :]
    offsets = jnp.where((rows == first_row)[:, None] & slot_zero, reach, offsets)
    offsets = jnp.where((rows == second_row)[:, None] & slot_zero, -reach, offsets)
    return ((rows[:, None] + offsets) % NC).astype(jnp.int32)


def draw_positions(key, part):
    spread = jnp.clip(jax.random.normal(jax.random.fold_in(key, 21), (NC, 3, CL), jnp.float32), -6.0, 6.0)
    radius = 0.6 / (2.0 * math.sin(math.pi * 2.0 * CT / NC))
    angle = 2.0 * math.pi * jnp.arange(NC, dtype=jnp.float32) / NC
    centre = jnp.stack([radius * jnp.cos(angle), radius * jnp.sin(angle), jnp.zeros((NC,), jnp.float32)], axis=1)
    return (spread + centre[:, :, None]).astype(jnp.float32)


def level_of(stream_key, extent, shards, smallest, high):
    gain, own = 1.0, jax.random.fold_in(stream_key, 6)
    for axis_at, parts in shards:
        steps = jnp.exp(jax.random.uniform(jax.random.fold_in(own, axis_at), (parts,), jnp.float32, smallest / len(shards), high / len(shards)))
        gain = gain * jnp.repeat(steps, extent[axis_at] // parts).reshape([-1 if axis == axis_at else 1 for axis in range(len(extent))])
    return gain


def profile(number_of, total, most, lean):
    loads = [(1 << 20) // math.isqrt(standing ** lean) + 1 for standing in range(2, number_of + 1)]
    rest, counts = total - most - (number_of - 1), [1] * (number_of - 1)
    while rest > 0:
        free = [i for i in range(number_of - 1) if counts[i] < most]
        whole, budget = sum([loads[i] for i in free]), rest
        for i in free:
            addition = min(most - counts[i], max(1, budget * loads[i] // whole), rest)
            counts[i] = counts[i] + addition
            rest = rest - addition
    return np.array([most] + counts)


def ragged_sizes(own_key, amount, total, bound, lean):
    if amount == 2:
        one = jax.random.randint(own_key, (), max(1, total - bound), min(bound, total - 1) + 1)
        return jnp.stack([one, total - one])
    tallies = jnp.asarray(profile(amount, total, bound, lean), jnp.int32)
    twos = (amount - 1) // 2
    source_of, taker = tallies[1:1 + 2 * twos:2], tallies[2:2 + 2 * twos:2]
    room = jnp.minimum(source_of - 1, bound - taker)
    shifted = jax.random.randint(jax.random.fold_in(own_key, 1), (twos,), 0, 1 << 20) % (room + 1)
    tallies = tallies.at[1:1 + 2 * twos:2].set(source_of - shifted).at[2:2 + 2 * twos:2].set(taker + shifted)
    return tallies[jax.random.permutation(jax.random.fold_in(own_key, 2), amount)]


def centred(key, dims, scale, most, shards=(), kind=jnp.bfloat16):
    loudness = level_of(key, dims, shards, -0.22, 0.18) if shards else 1.0
    entries = jax.random.normal(key, dims, jnp.float32) * scale * loudness
    return jnp.minimum(jnp.maximum(entries, -most), most).astype(kind)


def setup_inputs(seed: int = 0, part: int = 0) -> dict:
    key_of = jax.random.split(jax.random.key(seed), 7)
    part_splits = jax.random.split(jax.random.fold_in(key_of[6], part), 7)
    probe = centred(part_splits[0], (NC, PROBE, CL), 1.0, 6.0, ((0, 8),))
    positions = draw_positions(jax.random.fold_in(jax.random.fold_in(key_of[6], part), 71), part)
    conductivity = jnp.clip(jnp.exp(math.log(2.0) - 1.3862944 * jax.random.uniform(part_splits[2], (NC, CL), jnp.float32) ** level_of(part_splits[2], (NC, CL), ((0, 8),), -0.2, 0.2)), 0.5, 2.0)
    fluid_exchange = jnp.clip(jnp.exp(math.log(8.0) - 2.7725887 * jax.random.uniform(part_splits[3], (NC, CL), jnp.float32) ** level_of(part_splits[3], (NC, CL), ((0, 8),), -0.2, 0.2)), 0.5, 8.0)
    row_blocks = ragged_sizes(part_splits[4], NC, MEANB * NC, MAXB, 2).astype(jnp.int32)
    column_blocks = draw_column_blocks(jax.random.fold_in(jax.random.fold_in(key_of[6], part), 71), part)
    return dict(probe=probe, positions=positions, conductivity=conductivity, fluid_exchange=fluid_exchange, row_blocks=row_blocks, column_blocks=column_blocks)


WIDTH_SQ = 0.245
CENTER = 1.05
HALF_SPAN = 0.95


def conductance(row_pos, row_kappa, col_pos, col_kappa):
    offset = row_pos[..., :, :, None] - col_pos[..., :, None, :]
    dist_sq = jnp.sum(offset * offset, axis=-3)
    left = row_kappa[..., :, None]
    right = col_kappa[..., None, :]
    return 2.0 * left * right / (left + right) * jnp.exp(-dist_sq / WIDTH_SQ)


def apply_rows(probe_values, positions, conductivity, row_blocks, column_blocks):
    slot_ids = jnp.arange(MAXB, dtype=jnp.int32)
    diagonal_mask = jnp.eye(CL, dtype=bool)

    def row_terms(row_index):
        col_ids = column_blocks[row_index]
        conduct = conductance(positions[row_index][None], conductivity[row_index][None], positions[col_ids], conductivity[col_ids])
        active = (slot_ids < row_blocks[row_index])[:, None, None]
        itself = (col_ids == row_index)[:, None, None] & diagonal_mask[None]
        conduct = jnp.where(active & jnp.logical_not(itself), conduct, jnp.float32(0.0))
        degree = jnp.sum(conduct, axis=(0, 2))
        rounded = lax.optimization_barrier(conduct.astype(jnp.bfloat16))
        tile_values = rounded.astype(jnp.float32)
        gathered = probe_values[col_ids].astype(jnp.float32)
        product = jnp.einsum("sij,smj->mi", tile_values, gathered)
        return product, degree

    return lax.map(row_terms, jnp.arange(NC, dtype=jnp.int32))


def reference(probe, positions, conductivity, fluid_exchange, row_blocks, column_blocks):
    def operate(current):
        probe_values = current.astype(jnp.bfloat16)
        product, degree = apply_rows(probe_values, positions, conductivity, row_blocks, column_blocks)
        return current - product / (fluid_exchange + degree)[:, None, :]

    previous = probe.astype(jnp.float32)
    current = (operate(previous) - CENTER * previous) / HALF_SPAN
    for iteration in range(DEGREE - 1):
        following = 2.0 * (operate(current) - CENTER * current) / HALF_SPAN - previous
        previous, current = current, following
    return current
```

```python
import functools
import math

import jax
import jax.numpy as jnp
from jax import lax
from jax.experimental import pallas as pl
from jax.experimental.pallas import tpu as pltpu
from jax.sharding import PartitionSpec as P

DEGREE = 8
WIDTH_SQ = 0.245
CENTER = 1.05
HALF_SPAN = 0.95
SCALE = math.sqrt(math.log2(math.e) / WIDTH_SQ)
MESH = pl.DeviceIdType.MESH
REACHES = (-2, -1, 1, 2)


def kernel(
    teams, probe, pos, cond, fluid, counts, cols, out,
    geo, bcast, tiles, even, odd, cur, prev, inv, corr, ids, other,
    geo_send, geo_recv, win_send, win_recv, pair_send, pair_recv,
):
    rows, columns, particles = probe.shape
    half = columns // 2
    slots = cols.shape[1]
    clusters = teams * rows
    group = lax.axis_index("groups")
    member = lax.axis_index("team")
    team = lax.axis_index("blk")

    def at(reach):
        return (group, member, lax.rem(team + reach + teams, teams))

    partner = (group, 1 - member, team)
    barrier = pltpu.get_barrier_semaphore()
    for reach in REACHES:
        pl.semaphore_signal(barrier, inc=1, device_id=at(reach), device_id_type=MESH)
    pl.semaphore_signal(barrier, inc=1, device_id=partner, device_id_type=MESH)

    for r in range(rows):
        geo[2, r, 0:3, :] = pos[r] * SCALE
        geo[2, r, 3:4, :] = 0.5 / cond[r : r + 1, :]
        geo[2, r, 4:8, :] = jnp.zeros((4, particles), jnp.float32)
        mine = probe[r, pl.ds(pl.multiple_of(member * half, half), half), :]
        even[2 * rows + r] = mine
        cur[r] = mine.astype(jnp.float32)
        prev[r] = jnp.zeros((half, particles), jnp.float32)
    pl.semaphore_wait(barrier, len(REACHES) + 1)

    def geo_copy(n):
        reach = REACHES[n]
        return pltpu.make_async_remote_copy(
            src_ref=geo.at[2], dst_ref=geo.at[2 - reach],
            send_sem=geo_send.at[n], recv_sem=geo_recv.at[n],
            device_id=at(reach), device_id_type=MESH,
        )

    def win_copy(parity, n):
        reach = REACHES[n]
        window = (even, odd)[parity]
        return pltpu.make_async_remote_copy(
            src_ref=window.at[pl.ds(2 * rows, rows)], dst_ref=window.at[pl.ds((2 - reach) * rows, rows)],
            send_sem=win_send.at[parity, n], recv_sem=win_recv.at[parity, n],
            device_id=at(reach), device_id_type=MESH,
        )

    for n in range(4):
        geo_copy(n).start()
    for n in range(4):
        win_copy(0, n).start()

    def spread(place):
        def one(r, carry):
            turned = geo[place, r].T
            for k in range(4):
                bcast[place * rows + r, k] = jnp.broadcast_to(
                    turned[:, k : k + 1], (particles, particles)
                )
            return carry
        lax.fori_loop(0, rows, one, 0)

    spread(2)
    for n in range(4):
        geo_copy(n).wait()
        spread(2 - REACHES[n])

    base = (team - 2) * rows

    def build_row(r, carry):
        own = team * rows + r
        count = counts[r]
        xi = [jnp.broadcast_to(geo[2, r, k : k + 1, :], (8, particles)) for k in range(4)]

        def build_tile(s, state):
            total, selves = state
            col = cols[r, s]
            active = s < count
            place = col - base
            place = jnp.where(place < 0, place + clusters, place)
            place = jnp.where(place >= clusters, place - clusters, place)
            place = jnp.where(active, jnp.minimum(place, 5 * rows - 1), 0)
            ids[r, s] = place
            selves = selves + jnp.where(active & (col == own), 1.0, 0.0)
            bias = jnp.where(active, 0.0, -1e30)
            for j in range(0, particles, 16):
                parts = []
                for h in (j, j + 8):
                    dx = bcast[place, 0, h : h + 8, :] - xi[0]
                    dy = bcast[place, 1, h : h + 8, :] - xi[1]
                    dz = bcast[place, 2, h : h + 8, :] - xi[2]
                    power = bias - dx * dx - dy * dy - dz * dz
                    value = jnp.exp2(power) / (bcast[place, 3, h : h + 8, :] + xi[3])
                    total = total + value
                    parts.append(value)
                tiles[r, pl.ds(pl.multiple_of(s * particles + j, 16), 16), :] = jnp.concatenate(
                    parts, 0
                ).astype(jnp.bfloat16)
            return total, selves

        total, selves = lax.fori_loop(
            0, slots, build_tile, (jnp.zeros((8, particles), jnp.float32), jnp.float32(0.0))
        )
        itself = 1.0 / (xi[3] + xi[3])
        degree = jnp.sum(total, axis=0, keepdims=True) - selves * itself[0:1]
        divisor = fluid[pl.ds(r, 1), :] + degree
        inv[r] = jnp.broadcast_to((2.0 / HALF_SPAN) / divisor, (half, particles))
        rounded = itself[0:1].astype(jnp.bfloat16).astype(jnp.float32)
        corr[r] = jnp.broadcast_to(selves * rounded, (half, particles))
        return carry

    lax.fori_loop(0, rows, build_row, 0)

    def step(k, now):
        later = 1 - now
        window, target = (even, odd)[now], (even, odd)[later]
        for n in range(4):
            win_copy(now, n).wait()
        gain = jnp.where(k == 0, 0.5, 1.0)

        def row(r, inner):
            taken = jnp.concatenate(
                [window[ids[r, s]] for s in range(slots)],
                axis=1,
            )
            product = jnp.dot(taken, tiles[r], preferred_element_type=jnp.float32)
            mine = window[2 * rows + r].astype(jnp.float32)
            product = product - corr[r] * mine
            field = cur[r]
            change = (2.0 * (1.0 - CENTER) / HALF_SPAN) * field - product * inv[r]
            fresh = gain * change - prev[r]
            prev[r] = field
            cur[r] = fresh
            target[2 * rows + r] = fresh.astype(jnp.bfloat16)
            return inner

        lax.fori_loop(0, rows, row, 0, unroll=2)

        @pl.when(k < DEGREE - 1)
        def _():
            for n in range(4):
                win_copy(later, n).start()

    def two_steps(i, carry):
        step(2 * i, 0)
        step(2 * i + 1, 1)
        return carry

    lax.fori_loop(0, DEGREE // 2, two_steps, 0)

    swap = pltpu.make_async_remote_copy(
        src_ref=cur, dst_ref=other, send_sem=pair_send, recv_sem=pair_recv,
        device_id=partner, device_id_type=MESH,
    )
    swap.start()
    out[:, pl.ds(pl.multiple_of(member * half, half), half), :] = cur[...]
    swap.wait()
    out[:, pl.ds(pl.multiple_of((1 - member) * half, half), half), :] = other[...]


def local(teams, probe, positions, conductivity, fluid_exchange, row_blocks, column_blocks):
    rows, columns, particles = probe.shape
    slots = column_blocks.shape[1]
    half = columns // 2
    vmem = pl.BlockSpec(memory_space=pltpu.VMEM)
    smem = pl.BlockSpec(memory_space=pltpu.SMEM)
    f32 = jnp.float32
    return pl.pallas_call(
        functools.partial(kernel, teams),
        out_shape=jax.ShapeDtypeStruct((rows, columns, particles), f32),
        in_specs=[vmem, vmem, vmem, vmem, smem, smem],
        out_specs=vmem,
        scratch_shapes=[
            pltpu.VMEM((5, rows, 8, particles), f32),
            pltpu.VMEM((5 * rows, 4, particles, particles), f32),
            pltpu.VMEM((rows, slots * particles, particles), jnp.bfloat16),
            pltpu.VMEM((5 * rows, half, particles), jnp.bfloat16),
            pltpu.VMEM((5 * rows, half, particles), jnp.bfloat16),
            pltpu.VMEM((rows, half, particles), f32),
            pltpu.VMEM((rows, half, particles), f32),
            pltpu.VMEM((rows, half, particles), f32),
            pltpu.VMEM((rows, half, particles), f32),
            pltpu.SMEM((rows, slots), jnp.int32),
            pltpu.VMEM((rows, half, particles), f32),
            pltpu.SemaphoreType.DMA((4,)),
            pltpu.SemaphoreType.DMA((4,)),
            pltpu.SemaphoreType.DMA((2, 4)),
            pltpu.SemaphoreType.DMA((2, 4)),
            pltpu.SemaphoreType.DMA,
            pltpu.SemaphoreType.DMA,
        ],
        compiler_params=pltpu.CompilerParams(
            collective_id=0, has_side_effects=True, vmem_limit_bytes=48 * 1024 * 1024
        ),
    )(probe, positions, conductivity, fluid_exchange, row_blocks, column_blocks)


def solution(mesh):
    return jax.shard_map(
        functools.partial(local, mesh.shape["blk"]),
        mesh=mesh,
        in_specs=(
            P(("groups", "blk"), None, None),
            P(("groups", "blk"), None, None),
            P(("groups", "blk"), None),
            P(("groups", "blk"), None),
            P(("groups", "blk")),
            P(("groups", "blk"), None),
        ),
        out_specs=P(("groups", "blk"), None, None),
        check_vma=False,
    )
```

```python
import functools
import math

import jax
import jax.numpy as jnp
from jax import lax
from jax.experimental import pallas as pl
from jax.experimental.pallas import tpu as pltpu
from jax.sharding import PartitionSpec as P

DEGREE = 8
WIDTH_SQ = 0.245
CENTER = 1.05
HALF_SPAN = 0.95
SCALE = math.sqrt(math.log2(math.e) / WIDTH_SQ)
MESH = pl.DeviceIdType.MESH
REACHES = (-2, -1, 1, 2)
CHUNK = 4


def kernel(
    teams, probe, pos, cond, fluid, counts, cols, out,
    geo, bcast, tiles, even, odd, cur, prev, inv, corr, ids, other,
    geo_send, geo_recv, win_send, win_recv, pair_send, pair_recv,
):
    rows, columns, particles = probe.shape
    half = columns // 2
    slots = cols.shape[1]
    clusters = teams * rows
    group = lax.axis_index("groups")
    member = lax.axis_index("team")
    team = lax.axis_index("blk")

    def at(reach):
        return (group, member, lax.rem(team + reach + teams, teams))

    partner = (group, 1 - member, team)
    barrier = pltpu.get_barrier_semaphore()
    for reach in REACHES:
        pl.semaphore_signal(barrier, inc=1, device_id=at(reach), device_id_type=MESH)
    pl.semaphore_signal(barrier, inc=1, device_id=partner, device_id_type=MESH)

    for r in range(rows):
        geo[2, r, 0:3, :] = pos[r] * SCALE
        geo[2, r, 3:4, :] = 0.5 / cond[r : r + 1, :]
        geo[2, r, 4:8, :] = jnp.zeros((4, particles), jnp.float32)
        mine = probe[r, pl.ds(pl.multiple_of(member * half, half), half), :]
        even[2 * rows + r] = mine
        cur[r] = mine.astype(jnp.float32)
        prev[r] = jnp.zeros((half, particles), jnp.float32)
    pl.semaphore_wait(barrier, len(REACHES) + 1)

    def geo_copy(n):
        reach = REACHES[n]
        return pltpu.make_async_remote_copy(
            src_ref=geo.at[2], dst_ref=geo.at[2 - reach],
            send_sem=geo_send.at[n], recv_sem=geo_recv.at[n],
            device_id=at(reach), device_id_type=MESH,
        )

    def win_copy(parity, n, first=0, size=None):
        reach = REACHES[n]
        window = (even, odd)[parity]
        size = rows if size is None else size
        return pltpu.make_async_remote_copy(
            src_ref=window.at[pl.ds(2 * rows + first, size)], dst_ref=window.at[pl.ds((2 - reach) * rows + first, size)],
            send_sem=win_send.at[parity, n], recv_sem=win_recv.at[parity, n],
            device_id=at(reach), device_id_type=MESH,
        )

    for n in range(4):
        geo_copy(n).start()
    for n in range(4):
        win_copy(0, n).start()

    def spread(place):
        def one(r, carry):
            for k in range(4):
                line = geo[place, r, k : k + 1, :]
                bcast[place * rows + r, k] = jnp.broadcast_to(line, (particles, particles)).T
            return carry
        lax.fori_loop(0, rows, one, 0, unroll=2)

    spread(2)
    for n in range(4):
        geo_copy(n).wait()
        spread(2 - REACHES[n])

    base = (team - 2) * rows

    def build_row(r, carry):
        own = team * rows + r
        count = counts[r]
        xi = [jnp.broadcast_to(geo[2, r, k : k + 1, :], (8, particles)) for k in range(4)]

        def build_tile(s, state):
            total, selves = state
            col = cols[r, s]
            active = s < count
            place = col - base
            place = jnp.where(place < 0, place + clusters, place)
            place = jnp.where(place >= clusters, place - clusters, place)
            place = jnp.where(active, jnp.minimum(place, 5 * rows - 1), 0)
            ids[r, s] = place
            selves = selves + jnp.where(active & (col == own), 1.0, 0.0)
            bias = jnp.where(active, 0.0, -1e30)
            for j in range(0, particles, 16):
                parts = []
                for h in (j, j + 8):
                    dx = bcast[place, 0, h : h + 8, :] - xi[0]
                    dy = bcast[place, 1, h : h + 8, :] - xi[1]
                    dz = bcast[place, 2, h : h + 8, :] - xi[2]
                    power = bias - dx * dx - dy * dy - dz * dz
                    value = jnp.exp2(power) / (bcast[place, 3, h : h + 8, :] + xi[3])
                    total = total + value
                    parts.append(value)
                tiles[r, pl.ds(pl.multiple_of(s * particles + j, 16), 16), :] = jnp.concatenate(
                    parts, 0
                ).astype(jnp.bfloat16)
            return total, selves

        total, selves = lax.fori_loop(
            0, slots, build_tile, (jnp.zeros((8, particles), jnp.float32), jnp.float32(0.0)),
            unroll=3,
        )
        itself = 1.0 / (xi[3] + xi[3])
        degree = jnp.sum(total, axis=0, keepdims=True) - selves * itself[0:1]
        divisor = fluid[pl.ds(r, 1), :] + degree
        inv[r] = jnp.broadcast_to((2.0 / HALF_SPAN) / divisor, (half, particles))
        rounded = itself[0:1].astype(jnp.bfloat16).astype(jnp.float32)
        corr[r] = jnp.broadcast_to(selves * rounded, (half, particles))
        return carry

    lax.fori_loop(0, rows, build_row, 0)

    def step(k, now):
        later = 1 - now
        window, target = (even, odd)[now], (even, odd)[later]
        for n in range(4):
            win_copy(now, n).wait()
        gain = jnp.where(k == 0, 0.5, 1.0)

        def row(r):
            taken = jnp.concatenate(
                [window[ids[r, s]] for s in range(slots)],
                axis=1,
            )
            product = jnp.dot(taken, tiles[r], preferred_element_type=jnp.float32)
            mine = window[2 * rows + r].astype(jnp.float32)
            product = product - corr[r] * mine
            field = cur[r]
            change = (2.0 * (1.0 - CENTER) / HALF_SPAN) * field - product * inv[r]
            fresh = gain * change - prev[r]
            prev[r] = field
            cur[r] = fresh
            target[2 * rows + r] = fresh.astype(jnp.bfloat16)

        for first in range(0, rows, CHUNK):
            size = min(CHUNK, rows - first)
            for r in range(first, first + size):
                row(r)

            @pl.when(k < DEGREE - 1)
            def _():
                for n in range(4):
                    win_copy(later, n, first, size).start()

    def two_steps(i, carry):
        step(2 * i, 0)
        step(2 * i + 1, 1)
        return carry

    lax.fori_loop(0, DEGREE // 2, two_steps, 0)

    swap = pltpu.make_async_remote_copy(
        src_ref=cur, dst_ref=other, send_sem=pair_send, recv_sem=pair_recv,
        device_id=partner, device_id_type=MESH,
    )
    swap.start()
    out[:, pl.ds(pl.multiple_of(member * half, half), half), :] = cur[...]
    swap.wait()
    out[:, pl.ds(pl.multiple_of((1 - member) * half, half), half), :] = other[...]


def local(teams, probe, positions, conductivity, fluid_exchange, row_blocks, column_blocks):
    rows, columns, particles = probe.shape
    slots = column_blocks.shape[1]
    half = columns // 2
    vmem = pl.BlockSpec(memory_space=pltpu.VMEM)
    smem = pl.BlockSpec(memory_space=pltpu.SMEM)
    f32 = jnp.float32
    return pl.pallas_call(
        functools.partial(kernel, teams),
        out_shape=jax.ShapeDtypeStruct((rows, columns, particles), f32),
        in_specs=[vmem, vmem, vmem, vmem, smem, smem],
        out_specs=vmem,
        scratch_shapes=[
            pltpu.VMEM((5, rows, 8, particles), f32),
            pltpu.VMEM((5 * rows, 4, particles, particles), f32),
            pltpu.VMEM((rows, slots * particles, particles), jnp.bfloat16),
            pltpu.VMEM((5 * rows, half, particles), jnp.bfloat16),
            pltpu.VMEM((5 * rows, half, particles), jnp.bfloat16),
            pltpu.VMEM((rows, half, particles), f32),
            pltpu.VMEM((rows, half, particles), f32),
            pltpu.VMEM((rows, half, particles), f32),
            pltpu.VMEM((rows, half, particles), f32),
            pltpu.SMEM((rows, slots), jnp.int32),
            pltpu.VMEM((rows, half, particles), f32),
            pltpu.SemaphoreType.DMA((4,)),
            pltpu.SemaphoreType.DMA((4,)),
            pltpu.SemaphoreType.DMA((2, 4)),
            pltpu.SemaphoreType.DMA((2, 4)),
            pltpu.SemaphoreType.DMA,
            pltpu.SemaphoreType.DMA,
        ],
        compiler_params=pltpu.CompilerParams(
            collective_id=0, has_side_effects=True, vmem_limit_bytes=48 * 1024 * 1024
        ),
    )(probe, positions, conductivity, fluid_exchange, row_blocks, column_blocks)


def solution(mesh):
    return jax.shard_map(
        functools.partial(local, mesh.shape["blk"]),
        mesh=mesh,
        in_specs=(
            P(("groups", "blk"), None, None),
            P(("groups", "blk"), None, None),
            P(("groups", "blk"), None),
            P(("groups", "blk"), None),
            P(("groups", "blk")),
            P(("groups", "blk"), None),
        ),
        out_specs=P(("groups", "blk"), None, None),
        check_vma=False,
    )
```

```python
import functools
import math

import jax
import jax.numpy as jnp
from jax import lax
from jax.experimental import pallas as pl
from jax.experimental.pallas import tpu as pltpu
from jax.sharding import PartitionSpec as P

DEGREE = 8
WIDTH_SQ = 0.245
CENTER = 1.05
HALF_SPAN = 0.95
SCALE = math.sqrt(math.log2(math.e) / WIDTH_SQ)
MESH = pl.DeviceIdType.MESH
REACHES = (-2, -1, 1, 2)
CHUNK = 3


def kernel(
    teams, probe_in, pos_in, cond_in, fluid_in, counts_in, cols_in, out,
    probe, pos, cond, fluid, counts, cols, load_sem,
    geo, bcast, tiles, even, odd, cur, prev, inv, corr, ids, other,
    geo_send, geo_recv, win_send, win_recv, pair_send, pair_recv,
):
    loads = [
        pltpu.make_async_copy(source, place, load_sem.at[n])
        for n, (source, place) in enumerate(
            (
                (pos_in, pos), (cond_in, cond), (probe_in, probe),
                (cols_in, cols), (counts_in, counts), (fluid_in, fluid),
            )
        )
    ]
    for load in loads:
        load.start()
    rows, columns, particles = probe.shape
    half = columns // 2
    slots = cols.shape[1]
    clusters = teams * rows
    group = lax.axis_index("groups")
    member = lax.axis_index("team")
    team = lax.axis_index("blk")

    def at(reach):
        return (group, member, lax.rem(team + reach + teams, teams))

    partner = (group, 1 - member, team)
    barrier = pltpu.get_barrier_semaphore()
    for reach in REACHES:
        pl.semaphore_signal(barrier, inc=1, device_id=at(reach), device_id_type=MESH)
    pl.semaphore_signal(barrier, inc=1, device_id=partner, device_id_type=MESH)

    for load in loads[:3]:
        load.wait()
    for r in range(rows):
        geo[2, r, 0:3, :] = pos[r] * SCALE
        geo[2, r, 3:4, :] = 0.5 / cond[r : r + 1, :]
        geo[2, r, 4:8, :] = jnp.zeros((4, particles), jnp.float32)
        mine = probe[r, pl.ds(pl.multiple_of(member * half, half), half), :]
        even[2 * rows + r] = mine
        cur[r] = mine.astype(jnp.float32)
        prev[r] = jnp.zeros((half, particles), jnp.float32)
    pl.semaphore_wait(barrier, len(REACHES) + 1)

    def geo_copy(n):
        reach = REACHES[n]
        return pltpu.make_async_remote_copy(
            src_ref=geo.at[2], dst_ref=geo.at[2 - reach],
            send_sem=geo_send.at[n], recv_sem=geo_recv.at[n],
            device_id=at(reach), device_id_type=MESH,
        )

    def win_copy(parity, n, first=0, size=None):
        reach = REACHES[n]
        window = (even, odd)[parity]
        size = rows if size is None else size
        return pltpu.make_async_remote_copy(
            src_ref=window.at[pl.ds(2 * rows + first, size)], dst_ref=window.at[pl.ds((2 - reach) * rows + first, size)],
            send_sem=win_send.at[parity, n], recv_sem=win_recv.at[parity, n],
            device_id=at(reach), device_id_type=MESH,
        )

    for n in range(4):
        geo_copy(n).start()
    for n in range(4):
        win_copy(0, n).start()

    def spread(place):
        def one(r, carry):
            for k in range(4):
                line = geo[place, r, k : k + 1, :]
                bcast[place * rows + r, k] = jnp.broadcast_to(line, (particles, particles)).T
            return carry
        lax.fori_loop(0, rows, one, 0, unroll=2)

    spread(2)
    for n in range(4):
        geo_copy(n).wait()
        spread(2 - REACHES[n])

    for load in loads[3:]:
        load.wait()
    base = (team - 2) * rows

    def build_row(r, carry):
        own = team * rows + r
        count = counts[r]
        xi = [jnp.broadcast_to(geo[2, r, k : k + 1, :], (8, particles)) for k in range(4)]

        def build_tile(s, state):
            total, selves = state
            col = cols[r, s]
            active = s < count
            place = col - base
            place = jnp.where(place < 0, place + clusters, place)
            place = jnp.where(place >= clusters, place - clusters, place)
            place = jnp.where(active, jnp.minimum(place, 5 * rows - 1), 0)
            ids[r, s] = place
            selves = selves + jnp.where(active & (col == own), 1.0, 0.0)
            bias = jnp.where(active, 0.0, -1e30)
            for j in range(0, particles, 16):
                parts = []
                for h in (j, j + 8):
                    dx = bcast[place, 0, h : h + 8, :] - xi[0]
                    dy = bcast[place, 1, h : h + 8, :] - xi[1]
                    dz = bcast[place, 2, h : h + 8, :] - xi[2]
                    power = bias - dx * dx - dy * dy - dz * dz
                    value = jnp.exp2(power) / (bcast[place, 3, h : h + 8, :] + xi[3])
                    total = total + value
                    parts.append(value)
                tiles[r, pl.ds(pl.multiple_of(s * particles + j, 16), 16), :] = jnp.concatenate(
                    parts, 0
                ).astype(jnp.bfloat16)
            return total, selves

        total, selves = lax.fori_loop(
            0, slots, build_tile, (jnp.zeros((8, particles), jnp.float32), jnp.float32(0.0)),
            unroll=3,
        )
        itself = 1.0 / (xi[3] + xi[3])
        degree = jnp.sum(total, axis=0, keepdims=True) - selves * itself[0:1]
        divisor = fluid[pl.ds(r, 1), :] + degree
        inv[r] = jnp.broadcast_to((2.0 / HALF_SPAN) / divisor, (half, particles))
        rounded = itself[0:1].astype(jnp.bfloat16).astype(jnp.float32)
        corr[r] = jnp.broadcast_to(selves * rounded, (half, particles))
        return carry

    lax.fori_loop(0, rows, build_row, 0)

    def step(k, now):
        later = 1 - now
        window, target = (even, odd)[now], (even, odd)[later]
        for n in range(4):
            win_copy(now, n).wait()
        gain = jnp.where(k == 0, 0.5, 1.0)

        def row(r):
            taken = jnp.concatenate(
                [window[ids[r, s]] for s in range(slots)],
                axis=1,
            )
            product = jnp.dot(taken, tiles[r], preferred_element_type=jnp.float32)
            mine = window[2 * rows + r].astype(jnp.float32)
            product = product - corr[r] * mine
            field = cur[r]
            change = (2.0 * (1.0 - CENTER) / HALF_SPAN) * field - product * inv[r]
            fresh = gain * change - prev[r]
            prev[r] = field
            cur[r] = fresh
            target[2 * rows + r] = fresh.astype(jnp.bfloat16)

        for first in range(0, rows, CHUNK):
            size = min(CHUNK, rows - first)
            for r in range(first, first + size):
                row(r)

            @pl.when(k < DEGREE - 1)
            def _():
                for n in range(4):
                    win_copy(later, n, first, size).start()

    def two_steps(i, carry):
        step(2 * i, 0)
        step(2 * i + 1, 1)
        return carry

    lax.fori_loop(0, DEGREE // 2, two_steps, 0)

    swap = pltpu.make_async_remote_copy(
        src_ref=cur, dst_ref=other, send_sem=pair_send, recv_sem=pair_recv,
        device_id=partner, device_id_type=MESH,
    )
    swap.start()
    out[:, pl.ds(pl.multiple_of(member * half, half), half), :] = cur[...]
    swap.wait()
    out[:, pl.ds(pl.multiple_of((1 - member) * half, half), half), :] = other[...]


def local(teams, probe, positions, conductivity, fluid_exchange, row_blocks, column_blocks):
    rows, columns, particles = probe.shape
    slots = column_blocks.shape[1]
    half = columns // 2
    vmem = pl.BlockSpec(memory_space=pltpu.VMEM)
    anywhere = pl.BlockSpec(memory_space=pl.ANY)
    f32 = jnp.float32
    return pl.pallas_call(
        functools.partial(kernel, teams),
        out_shape=jax.ShapeDtypeStruct((rows, columns, particles), f32),
        in_specs=[anywhere] * 6,
        out_specs=vmem,
        scratch_shapes=[
            pltpu.VMEM(probe.shape, probe.dtype),
            pltpu.VMEM(positions.shape, f32),
            pltpu.VMEM(conductivity.shape, f32),
            pltpu.VMEM(fluid_exchange.shape, f32),
            pltpu.SMEM(row_blocks.shape, jnp.int32),
            pltpu.SMEM(column_blocks.shape, jnp.int32),
            pltpu.SemaphoreType.DMA((6,)),
            pltpu.VMEM((5, rows, 8, particles), f32),
            pltpu.VMEM((5 * rows, 4, particles, particles), f32),
            pltpu.VMEM((rows, slots * particles, particles), jnp.bfloat16),
            pltpu.VMEM((5 * rows, half, particles), jnp.bfloat16),
            pltpu.VMEM((5 * rows, half, particles), jnp.bfloat16),
            pltpu.VMEM((rows, half, particles), f32),
            pltpu.VMEM((rows, half, particles), f32),
            pltpu.VMEM((rows, half, particles), f32),
            pltpu.VMEM((rows, half, particles), f32),
            pltpu.SMEM((rows, slots), jnp.int32),
            pltpu.VMEM((rows, half, particles), f32),
            pltpu.SemaphoreType.DMA((4,)),
            pltpu.SemaphoreType.DMA((4,)),
            pltpu.SemaphoreType.DMA((2, 4)),
            pltpu.SemaphoreType.DMA((2, 4)),
            pltpu.SemaphoreType.DMA,
            pltpu.SemaphoreType.DMA,
        ],
        compiler_params=pltpu.CompilerParams(
            collective_id=0, has_side_effects=True, vmem_limit_bytes=60 * 1024 * 1024
        ),
    )(probe, positions, conductivity, fluid_exchange, row_blocks, column_blocks)


def solution(mesh):
    return jax.shard_map(
        functools.partial(local, mesh.shape["blk"]),
        mesh=mesh,
        in_specs=(
            P(("groups", "blk"), None, None),
            P(("groups", "blk"), None, None),
            P(("groups", "blk"), None),
            P(("groups", "blk"), None),
            P(("groups", "blk")),
            P(("groups", "blk"), None),
        ),
        out_specs=P(("groups", "blk"), None, None),
        check_vma=False,
    )
```

```python
import functools
import math

import jax
import jax.numpy as jnp
from jax import lax
from jax.experimental import pallas as pl
from jax.experimental.pallas import tpu as pltpu
from jax.sharding import PartitionSpec as P

DEGREE = 8
WIDTH_SQ = 0.245
CENTER = 1.05
HALF_SPAN = 0.95
SCALE = math.sqrt(math.log2(math.e) / WIDTH_SQ)
MESH = pl.DeviceIdType.MESH
REACHES = (-2, -1, 1, 2)
CHUNK = 3


def kernel(
    teams, probe_in, pos_in, cond_in, fluid_in, counts_in, cols_in, out,
    probe, pos, cond, fluid, counts, cols, load_sem,
    geo, bcast, tiles, even, odd, cur, prev, inv, corr, ids, other,
    geo_send, geo_recv, win_send, win_recv, pair_send, pair_recv,
):
    loads = [
        pltpu.make_async_copy(source, place, load_sem.at[n])
        for n, (source, place) in enumerate(
            (
                (pos_in, pos), (cond_in, cond), (probe_in, probe),
                (cols_in, cols), (counts_in, counts), (fluid_in, fluid),
            )
        )
    ]
    for load in loads:
        load.start()
    rows, columns, particles = probe.shape
    half = columns // 2
    slots = cols.shape[1]
    clusters = teams * rows
    group = lax.axis_index("groups")
    member = lax.axis_index("team")
    team = lax.axis_index("blk")

    def at(reach):
        return (group, member, lax.rem(team + reach + teams, teams))

    partner = (group, 1 - member, team)
    barrier = pltpu.get_barrier_semaphore()
    for reach in REACHES:
        pl.semaphore_signal(barrier, inc=1, device_id=at(reach), device_id_type=MESH)
    pl.semaphore_signal(barrier, inc=1, device_id=partner, device_id_type=MESH)

    for load in loads[:3]:
        load.wait()
    for r in range(rows):
        geo[2, r, 0:3, :] = pos[r] * SCALE
        geo[2, r, 3:4, :] = 0.5 / cond[r : r + 1, :]
        mine = probe[r, pl.ds(pl.multiple_of(member * half, half), half), :]
        even[2 * rows + r] = mine
        cur[r] = mine.astype(jnp.float32)
        prev[r] = jnp.zeros((half, particles), jnp.float32)
    pl.semaphore_wait(barrier, len(REACHES) + 1)

    def geo_copy(n):
        reach = REACHES[n]
        return pltpu.make_async_remote_copy(
            src_ref=geo.at[2], dst_ref=geo.at[2 - reach],
            send_sem=geo_send.at[n], recv_sem=geo_recv.at[n],
            device_id=at(reach), device_id_type=MESH,
        )

    def win_copy(parity, n, first=0, size=None):
        reach = REACHES[n]
        window = (even, odd)[parity]
        size = rows if size is None else size
        return pltpu.make_async_remote_copy(
            src_ref=window.at[pl.ds(2 * rows + first, size)], dst_ref=window.at[pl.ds((2 - reach) * rows + first, size)],
            send_sem=win_send.at[parity, n], recv_sem=win_recv.at[parity, n],
            device_id=at(reach), device_id_type=MESH,
        )

    for n in range(4):
        geo_copy(n).start()
    def spread(place):
        def one(r, carry):
            for k in range(4):
                line = geo[place, r, k : k + 1, :]
                bcast[place * rows + r, k] = jnp.broadcast_to(line, (particles, particles)).T
            return carry
        lax.fori_loop(0, rows, one, 0, unroll=2)

    spread(2)
    for n in range(4):
        geo_copy(n).wait()
        spread(2 - REACHES[n])
    for n in range(4):
        win_copy(0, n).start()

    for load in loads[3:]:
        load.wait()
    base = (team - 2) * rows

    def build_row(r, carry):
        own = team * rows + r
        count = counts[r]
        xi = [jnp.broadcast_to(geo[2, r, k : k + 1, :], (8, particles)) for k in range(4)]

        def build_tile(s, state):
            total, selves = state
            col = cols[r, s]
            active = s < count
            place = col - base
            place = jnp.where(place < 0, place + clusters, place)
            place = jnp.where(place >= clusters, place - clusters, place)
            place = jnp.where(active, jnp.minimum(place, 5 * rows - 1), 0)
            ids[r, s] = place
            selves = selves + jnp.where(active & (col == own), 1.0, 0.0)
            bias = jnp.where(active, 0.0, -1e30)
            for j in range(0, particles, 16):
                parts = []
                for h in (j, j + 8):
                    dx = bcast[place, 0, h : h + 8, :] - xi[0]
                    dy = bcast[place, 1, h : h + 8, :] - xi[1]
                    dz = bcast[place, 2, h : h + 8, :] - xi[2]
                    power = bias - dx * dx - dy * dy - dz * dz
                    value = jnp.exp2(power) / (bcast[place, 3, h : h + 8, :] + xi[3])
                    total = total + value
                    parts.append(value)
                tiles[r, pl.ds(pl.multiple_of(s * particles + j, 16), 16), :] = jnp.concatenate(
                    parts, 0
                ).astype(jnp.bfloat16)
            return total, selves

        total, selves = lax.fori_loop(
            0, slots, build_tile, (jnp.zeros((8, particles), jnp.float32), jnp.float32(0.0)),
            unroll=3,
        )
        itself = 1.0 / (xi[3] + xi[3])
        degree = jnp.sum(total, axis=0, keepdims=True) - selves * itself[0:1]
        divisor = fluid[pl.ds(r, 1), :] + degree
        inv[r] = jnp.broadcast_to((2.0 / HALF_SPAN) / divisor, (half, particles))
        rounded = itself[0:1].astype(jnp.bfloat16).astype(jnp.float32)
        corr[r] = jnp.broadcast_to(selves * rounded, (half, particles))
        return carry

    lax.fori_loop(0, rows, build_row, 0)

    def step(k, now):
        later = 1 - now
        window, target = (even, odd)[now], (even, odd)[later]
        for n in range(4):
            win_copy(now, n).wait()
        gain = jnp.where(k == 0, 0.5, 1.0)

        def row(r):
            taken = jnp.concatenate(
                [window[ids[r, s]] for s in range(slots)],
                axis=1,
            )
            product = jnp.dot(taken, tiles[r], preferred_element_type=jnp.float32)
            mine = window[2 * rows + r].astype(jnp.float32)
            product = product - corr[r] * mine
            field = cur[r]
            change = (2.0 * (1.0 - CENTER) / HALF_SPAN) * field - product * inv[r]
            fresh = gain * change - prev[r]
            prev[r] = field
            cur[r] = fresh
            target[2 * rows + r] = fresh.astype(jnp.bfloat16)

        for first in range(0, rows, CHUNK):
            size = min(CHUNK, rows - first)
            for r in range(first, first + size):
                row(r)

            @pl.when(k < DEGREE - 1)
            def _():
                for n in range(4):
                    win_copy(later, n, first, size).start()

    def two_steps(i, carry):
        step(2 * i, 0)
        step(2 * i + 1, 1)
        return carry

    lax.fori_loop(0, DEGREE // 2, two_steps, 0)

    swap = pltpu.make_async_remote_copy(
        src_ref=cur, dst_ref=other, send_sem=pair_send, recv_sem=pair_recv,
        device_id=partner, device_id_type=MESH,
    )
    swap.start()
    out[:, pl.ds(pl.multiple_of(member * half, half), half), :] = cur[...]
    swap.wait()
    out[:, pl.ds(pl.multiple_of((1 - member) * half, half), half), :] = other[...]


def local(teams, probe, positions, conductivity, fluid_exchange, row_blocks, column_blocks):
    rows, columns, particles = probe.shape
    slots = column_blocks.shape[1]
    half = columns // 2
    vmem = pl.BlockSpec(memory_space=pltpu.VMEM)
    anywhere = pl.BlockSpec(memory_space=pl.ANY)
    f32 = jnp.float32
    return pl.pallas_call(
        functools.partial(kernel, teams),
        out_shape=jax.ShapeDtypeStruct((rows, columns, particles), f32),
        in_specs=[anywhere] * 6,
        out_specs=vmem,
        scratch_shapes=[
            pltpu.VMEM(probe.shape, probe.dtype),
            pltpu.VMEM(positions.shape, f32),
            pltpu.VMEM(conductivity.shape, f32),
            pltpu.VMEM(fluid_exchange.shape, f32),
            pltpu.SMEM(row_blocks.shape, jnp.int32),
            pltpu.SMEM(column_blocks.shape, jnp.int32),
            pltpu.SemaphoreType.DMA((6,)),
            pltpu.VMEM((5, rows, 4, particles), f32),
            pltpu.VMEM((5 * rows, 4, particles, particles), f32),
            pltpu.VMEM((rows, slots * particles, particles), jnp.bfloat16),
            pltpu.VMEM((5 * rows, half, particles), jnp.bfloat16),
            pltpu.VMEM((5 * rows, half, particles), jnp.bfloat16),
            pltpu.VMEM((rows, half, particles), f32),
            pltpu.VMEM((rows, half, particles), f32),
            pltpu.VMEM((rows, half, particles), f32),
            pltpu.VMEM((rows, half, particles), f32),
            pltpu.SMEM((rows, slots), jnp.int32),
            pltpu.VMEM((rows, half, particles), f32),
            pltpu.SemaphoreType.DMA((4,)),
            pltpu.SemaphoreType.DMA((4,)),
            pltpu.SemaphoreType.DMA((2, 4)),
            pltpu.SemaphoreType.DMA((2, 4)),
            pltpu.SemaphoreType.DMA,
            pltpu.SemaphoreType.DMA,
        ],
        compiler_params=pltpu.CompilerParams(
            collective_id=0, has_side_effects=True, vmem_limit_bytes=60 * 1024 * 1024
        ),
    )(probe, positions, conductivity, fluid_exchange, row_blocks, column_blocks)


def solution(mesh):
    return jax.shard_map(
        functools.partial(local, mesh.shape["blk"]),
        mesh=mesh,
        in_specs=(
            P(("groups", "blk"), None, None),
            P(("groups", "blk"), None, None),
            P(("groups", "blk"), None),
            P(("groups", "blk"), None),
            P(("groups", "blk")),
            P(("groups", "blk"), None),
        ),
        out_specs=P(("groups", "blk"), None, None),
        check_vma=False,
    )
```
